128 devices in a mesh: outer: 16 (over x_lo, y, core), inner: 8 (over x_hi, z).
Axes of the slice: x: 4 (x_hi: 2, x_lo: 2; x = x_hi * 2 + x_lo), y: 4, z: 4, core: 2. Of those that a mesh axis runs over, the one named last changes fastest.
Arguments:
- queries: bfloat16 [16384, 6144], P(('outer', 'inner')), may hold values from -8 to 8
- compressed: bfloat16 [16384, 576], P(('outer', 'inner')), may hold values from -8 to 8
- kv_weight: bfloat16 [512, 8192], replicated, may hold values from -0.25 to 0.25
- segments: int32 [128], replicated, may hold values from 0 to 31, never falling along the last dimension, each value on 1 to 8 neighbouring positions
- grad_out: bfloat16 [16384, 4096], P(('outer', 'inner')), may hold values from -6 to 6
Outputs:
- attended: bfloat16 [16384, 4096], P(('outer', 'inner'))
- grad_queries: bfloat16 [16384, 6144], P(('outer', 'inner'))
- grad_compressed: bfloat16 [16384, 576], P(('outer', 'inner'))
- grad_weight_t: float32 [8192, 512], P(('outer', 'inner'))
The draws below stay inside these ranges and needn't reach their ends.
Inputs may be any that keep to these rules, and one draw needn't show every extreme that they name: `segments`: ids never fall along the sequence; every document covers 1 to 8 consecutive tiles and some document covers exactly 8.
All inputs are finite; a program needn't handle non-finite values.
Results may differ from the reference program's by a relative error of at most 0.014.
Values may be sent and summed in bfloat16 or wider, within the bound.
No kernel may reach another device: no remote copies, remote signals or barrier semaphores. Data moves between devices by JAX's collectives and lax.ppermute only.
A program may use at most 256 MiB of HBM per device.

```python
import math
import jax
import jax.numpy as jnp
import numpy as np
from jax import lax

LATENT = 512
NOPE = 128
ROPE = 64
VDIM = 128
HEADS = 32
TILE = 128
TOK_DEV = 128
TOKENS = 16384
TILES = 128
MOST_TILES = 8
DOCS = 32
N_INNER = 8


def draw_queries(key, part):
    key = jax.random.fold_in(key, 11)
    values = jnp.clip(jax.random.normal(key, (TOKENS, HEADS, NOPE + ROPE), jnp.float32), -8.0, 8.0)
    return values.reshape(TOKENS, HEADS * (NOPE + ROPE)).astype(jnp.bfloat16)


def draw_compressed(key, part):
    key = jax.random.fold_in(key, 23)
    latent_key, rope_key = jax.random.split(key, 2)
    latent = jnp.clip(jax.random.normal(latent_key, (TOKENS, LATENT), jnp.float32), -8.0, 8.0)
    rotary = jnp.clip(jax.random.normal(rope_key, (TOKENS, ROPE), jnp.float32), -8.0, 8.0)
    return jnp.concatenate([latent, rotary], axis=1).astype(jnp.bfloat16)


def levels(rng, extent, shards, low, top_value):
    loudness = 1.0
    for dim, shards_of in shards:
        steps = jax.random.uniform(jax.random.fold_in(jax.random.fold_in(rng, 6), dim), (shards_of,), jnp.float32, low / len(shards), top_value / len(shards))
        loudness = loudness * jnp.repeat(jnp.exp(steps), extent[dim] // shards_of).reshape((-1,) + (1,) * (len(extent) - 1 - dim))
    return loudness


def profile(amount, total, reach, lean):
    portions = [(1 << 20) // math.isqrt(rank ** lean) + 1 for rank in range(2, amount + 1)]
    spare, holding = total - reach - (amount - 1), [1] * (amount - 1)
    while spare > 0:
        free = [i for i in range(amount - 1) if holding[i] < reach]
        pool, budget = sum([portions[i] for i in free]), spare
        for i in free:
            extra = min(reach - holding[i], max(1, budget * portions[i] // pool), spare)
            holding[i] = holding[i] + extra
            spare = spare - extra
    return np.array([reach] + holding)


def uneven(own_key, amount, total, most, slope):
    if amount == 2:
        one = jax.random.randint(own_key, (), max(1, total - most), min(most, total - 1) + 1)
        return jnp.stack([one, total - one])
    tallies = jnp.asarray(profile(amount, total, most, slope), jnp.int32)
    pairs = (amount - 1) // 2
    source_of, receiver = tallies[1:1 + 2 * pairs:2], tallies[2:2 + 2 * pairs:2]
    slack = jnp.minimum(source_of - 1, most - receiver)
    passed = jax.random.randint(jax.random.fold_in(own_key, 1), (pairs,), 0, 1 << 20) % (slack + 1)
    tallies = tallies.at[1:1 + 2 * pairs:2].set(source_of - passed).at[2:2 + 2 * pairs:2].set(receiver + passed)
    return tallies[jax.random.permutation(jax.random.fold_in(own_key, 2), amount)]


def centred(own_key, shape, width, most, cuts=(), held_as=jnp.bfloat16):
    factor_of = levels(own_key, shape, cuts, -0.22, 0.18) if cuts else 1.0
    entries = jax.random.normal(own_key, shape, jnp.float32) * width * factor_of
    return jnp.minimum(jnp.maximum(entries, -most), most).astype(held_as)


def setup_inputs(seed: int = 0) -> dict:
    streams_of = jax.random.split(jax.random.key(seed), 6)
    return {
        "queries": draw_queries(jax.random.fold_in(streams_of[5], 71), 0),
        "compressed": draw_compressed(jax.random.fold_in(streams_of[5], 71), 0),
        "kv_weight": centred(streams_of[2], (LATENT, HEADS * (NOPE + VDIM)), LATENT ** -0.5, 0.25),
        "segments": jnp.searchsorted(jnp.cumsum(uneven(streams_of[3], DOCS, TILES, MOST_TILES, 2)), jnp.arange(TILES), side="right").astype(jnp.int32),
        "grad_out": centred(streams_of[4], (TOKENS, HEADS * VDIM), 1.0, 6.0, ((0, 128),)),
    }


def attend(query_heads, keys_values, key_rope, allowed, grad_heads, softmax_scale):
    query_nope = query_heads[:, :, :NOPE].astype(jnp.float32)
    query_rope = query_heads[:, :, NOPE:].astype(jnp.float32)
    key_nope = keys_values[:, :, :NOPE].astype(jnp.float32)
    values = keys_values[:, :, NOPE:].astype(jnp.float32)
    rope_keys = key_rope.astype(jnp.float32)
    grad_wide = grad_heads.astype(jnp.float32)
    scores = (jnp.einsum('thd,khd->htk', query_nope, key_nope) + jnp.einsum('thr,kr->htk', query_rope, rope_keys)) * softmax_scale
    masked = jnp.where(allowed[None], scores, -1e30)
    row_max = jnp.max(masked, axis=2, keepdims=True)
    weights_exp = jnp.where(allowed[None], jnp.exp(masked - row_max), 0.0)
    probs = weights_exp / jnp.sum(weights_exp, axis=2, keepdims=True)
    probs_half = probs.astype(jnp.bfloat16).astype(jnp.float32)
    attended = jnp.einsum('htk,khd->thd', probs_half, values).astype(jnp.bfloat16)
    grad_probs = jnp.einsum('thd,khd->htk', grad_wide, values)
    row_dot = jnp.sum(probs * grad_probs, axis=2, keepdims=True)
    grad_scores = (softmax_scale * probs * (grad_probs - row_dot)).astype(jnp.bfloat16).astype(jnp.float32)
    grad_nope = jnp.einsum('htk,khd->thd', grad_scores, key_nope)
    grad_rope = jnp.einsum('htk,kr->thr', grad_scores, rope_keys)
    grad_query = jnp.concatenate([grad_nope, grad_rope], axis=2).astype(jnp.bfloat16)
    key_term = jnp.einsum('htk,thd->khd', grad_scores, query_nope)
    value_term = jnp.einsum('htk,thd->khd', probs_half, grad_wide)
    grad_kv_term = jnp.concatenate([key_term, value_term], axis=2).astype(jnp.bfloat16)
    grad_rope_term = jnp.einsum('htk,thr->kr', grad_scores, query_rope).astype(jnp.bfloat16)
    return attended, grad_query, grad_kv_term, grad_rope_term


def reference(queries, compressed, kv_weight, segments, grad_out):
    softmax_scale = (NOPE + ROPE) ** -0.5
    window = N_INNER * TOK_DEV
    margin = window - TOK_DEV
    latent = compressed[:, :LATENT]
    key_rope = compressed[:, LATENT:]
    keys_values = jnp.dot(latent, kv_weight, preferred_element_type=jnp.float32).astype(jnp.bfloat16)
    keys_values = keys_values.reshape(TOKENS, HEADS, NOPE + VDIM)
    kv_padded = jnp.concatenate([jnp.zeros((margin, HEADS, NOPE + VDIM), jnp.bfloat16), keys_values], axis=0)
    rope_padded = jnp.concatenate([jnp.zeros((margin, ROPE), jnp.bfloat16), key_rope], axis=0)
    token_segment = jnp.repeat(segments, TILE)
    seg_padded = jnp.concatenate([jnp.full((margin,), -1, jnp.int32), token_segment], axis=0)
    query_heads = queries.reshape(TOKENS, HEADS, NOPE + ROPE)
    grad_heads = grad_out.reshape(TOKENS, HEADS, VDIM)

    def one_block(running, block_id):
        acc_kv, acc_rope = running
        first_row = (block_id * TOK_DEV).astype(jnp.int32)
        query_block = lax.dynamic_slice_in_dim(query_heads, first_row, TOK_DEV, 0)
        grad_block = lax.dynamic_slice_in_dim(grad_heads, first_row, TOK_DEV, 0)
        kv_block = lax.dynamic_slice_in_dim(kv_padded, first_row, window, 0)
        rope_block = lax.dynamic_slice_in_dim(rope_padded, first_row, window, 0)
        seg_keys = lax.dynamic_slice_in_dim(seg_padded, first_row, window, 0)
        seg_query = lax.dynamic_slice_in_dim(token_segment, first_row, TOK_DEV, 0)
        key_pos = first_row - margin + jnp.arange(window, dtype=jnp.int32)
        query_pos = first_row + jnp.arange(TOK_DEV, dtype=jnp.int32)
        allowed = (key_pos[None, :] <= query_pos[:, None]) & (seg_keys[None, :] == seg_query[:, None]) & (key_pos[None, :] >= 0)
        attended, grad_query, grad_kv_term, grad_rope_term = attend(query_block, kv_block, rope_block, allowed, grad_block, softmax_scale)
        old_kv = lax.dynamic_slice_in_dim(acc_kv, first_row, window, 0)
        acc_kv = lax.dynamic_update_slice_in_dim(acc_kv, old_kv + grad_kv_term.astype(jnp.float32), first_row, 0)
        old_rope = lax.dynamic_slice_in_dim(acc_rope, first_row, window, 0)
        acc_rope = lax.dynamic_update_slice_in_dim(acc_rope, old_rope + grad_rope_term.astype(jnp.float32), first_row, 0)
        return (acc_kv, acc_rope), (attended, grad_query)

    block_ids = jnp.arange(TOKENS // TOK_DEV, dtype=jnp.int32)
    initial = (jnp.zeros((margin + TOKENS, HEADS, NOPE + VDIM), jnp.float32), jnp.zeros((margin + TOKENS, ROPE), jnp.float32))
    (acc_kv, acc_rope), (attended, grad_query) = lax.scan(one_block, initial, block_ids)
    summed_kv = acc_kv[margin:].reshape(TOKENS, HEADS * (NOPE + VDIM))
    grad_rope = acc_rope[margin:].astype(jnp.bfloat16)
    weight_wide = kv_weight.astype(jnp.float32)
    grad_latent = jnp.dot(summed_kv, weight_wide.T, precision=lax.Precision.HIGHEST).astype(jnp.bfloat16)
    grad_compressed = jnp.concatenate([grad_latent, grad_rope], axis=1)
    grad_weight_t = jnp.dot(summed_kv.T, latent.astype(jnp.float32), precision=lax.Precision.HIGHEST)
    attended = attended.reshape(TOKENS, HEADS * VDIM)
    grad_query = grad_query.reshape(TOKENS, HEADS * (NOPE + ROPE))
    return attended, grad_query, grad_compressed, grad_weight_t
```

```python
import functools

import jax
import jax.numpy as jnp
from jax import lax
from jax.experimental import pallas as pl
from jax.experimental.pallas import tpu as pltpu
from jax.sharding import PartitionSpec as P

LATENT = 512
NOPE = 128
ROPE = 64
VDIM = 128
HEADS = 32
TILE = 128
QDIM = NOPE + ROPE
KVDIM = NOPE + VDIM
WIDE = LATENT + ROPE
STEP_HEADS = 4
CHUNKS = ((0, 4), (4, 4))
BF16 = jnp.bfloat16
F32 = jnp.float32

ROWS_ROWS = (((1,), (1,)), ((), ()))
COLS_COLS = (((0,), (0,)), ((), ()))


def dot(a, b):
    return jnp.dot(a, b, preferred_element_type=F32)


def dot_general(a, b, dims):
    return lax.dot_general(a, b, dims, preferred_element_type=F32)


def attend_kernel(core_ref, keys_ref, bias_ref, q_ref, g_ref, w_ref,
                  att_ref, gq_ref, keep_ref, send_ref, dkeys_ref, *, scale):
    tok = q_ref.shape[0]
    keys = keys_ref[...]
    latent = keys_ref[:, :LATENT]
    q_nope, q_cat, g_heads, g_abs = [], [], [], []
    for h in range(STEP_HEADS):
        qn = q_ref[:, h * QDIM:h * QDIM + NOPE]
        qr = q_ref[:, h * QDIM + NOPE:(h + 1) * QDIM]
        g = g_ref[:, h * VDIM:(h + 1) * VDIM]
        wk = w_ref[:, h * KVDIM:h * KVDIM + NOPE]
        wv = w_ref[:, h * KVDIM + NOPE:(h + 1) * KVDIM]
        qa = (dot_general(qn, wk, ROWS_ROWS) * scale).astype(BF16)
        qr = (qr.astype(F32) * scale).astype(BF16)
        q_nope.append(qn)
        q_cat.append(jnp.concatenate([qa, qr], axis=1))
        g_heads.append(g)
        g_abs.append(dot_general(g, wv, ROWS_ROWS).astype(BF16))
    q_cat = jnp.concatenate(q_cat, axis=0)
    g_abs = jnp.concatenate(g_abs, axis=0)
    scores = dot_general(q_cat, keys, ROWS_ROWS)
    grad_probs = dot_general(g_abs, latent, ROWS_ROWS)
    bias = bias_ref[...]
    probs_half, grad_scores = [], []
    for h in range(STEP_HEADS):
        s = scores[h * tok:(h + 1) * tok] + bias
        s = jnp.exp(s - jnp.max(s, axis=1, keepdims=True))
        p = s * (1.0 / jnp.sum(s, axis=1, keepdims=True))
        gp = grad_probs[h * tok:(h + 1) * tok]
        row_dot = jnp.sum(p * gp, axis=1, keepdims=True)
        probs_half.append(p.astype(BF16))
        grad_scores.append((p * (gp - row_dot)).astype(BF16))
    probs_half = jnp.concatenate(probs_half, axis=0)
    grad_scores = jnp.concatenate(grad_scores, axis=0)
    mixed = dot(probs_half, latent).astype(BF16)
    grad_mixed = dot(grad_scores, keys) * scale
    grad_mixed_lat = grad_mixed[:, :LATENT].astype(BF16)
    grad_rope = grad_mixed[:, LATENT:].astype(BF16)
    term = dot_general(grad_scores, q_cat, COLS_COLS)
    value_term = dot_general(probs_half, g_abs, COLS_COLS)

    @pl.when(pl.program_id(0) == 0)
    def _():
        dkeys_ref[...] = jnp.zeros_like(dkeys_ref)

    dkeys_ref[:, :LATENT] += term[:, :LATENT] + value_term
    dkeys_ref[:, LATENT:] += term[:, LATENT:]
    weight_terms = []
    for h in range(STEP_HEADS):
        rows = slice(h * tok, (h + 1) * tok)
        wk = w_ref[:, h * KVDIM:h * KVDIM + NOPE]
        wv = w_ref[:, h * KVDIM + NOPE:(h + 1) * KVDIM]
        att_ref[:, h * VDIM:(h + 1) * VDIM] = dot(mixed[rows], wv).astype(BF16)
        gq_ref[:, h * QDIM:h * QDIM + NOPE] = dot(grad_mixed_lat[rows], wk).astype(BF16)
        gq_ref[:, h * QDIM + NOPE:(h + 1) * QDIM] = grad_rope[rows]
        weight_terms.append(dot_general(q_nope[h], grad_mixed_lat[rows], COLS_COLS).astype(BF16))
        weight_terms.append(dot_general(g_heads[h], mixed[rows], COLS_COLS).astype(BF16))
    half = STEP_HEADS // 2 * 2
    first = jnp.concatenate(weight_terms[:half], axis=0).reshape(8, 1, 64, LATENT)
    second = jnp.concatenate(weight_terms[half:], axis=0).reshape(8, 1, 64, LATENT)

    @pl.when(core_ref[0] == 0)
    def _():
        keep_ref[...] = first
        send_ref[...] = second

    @pl.when(core_ref[0] != 0)
    def _():
        keep_ref[...] = second
        send_ref[...] = first


def attend_chunk(core, keys, bias, queries, grad_out, kv_weight, first, count, scale):
    tok = queries.shape[0]
    n_keys = keys.shape[0]
    whole = lambda s, c: (0, 0)
    column = lambda s, c: (0, first + s)
    own = lambda s, c: (0, s)
    block = lambda s, c: (0, s, 0, 0)
    heads = count * STEP_HEADS
    return pl.pallas_call(
        functools.partial(attend_kernel, scale=scale),
        grid_spec=pltpu.PrefetchScalarGridSpec(
            num_scalar_prefetch=1,
            grid=(count,),
            in_specs=[
                pl.BlockSpec((n_keys, WIDE), whole),
                pl.BlockSpec((tok, n_keys), whole),
                pl.BlockSpec((tok, STEP_HEADS * QDIM), column),
                pl.BlockSpec((tok, STEP_HEADS * VDIM), column),
                pl.BlockSpec((LATENT, STEP_HEADS * KVDIM), column),
            ],
            out_specs=[
                pl.BlockSpec((tok, STEP_HEADS * VDIM), own),
                pl.BlockSpec((tok, STEP_HEADS * QDIM), own),
                pl.BlockSpec((8, 1, 64, LATENT), block),
                pl.BlockSpec((8, 1, 64, LATENT), block),
                pl.BlockSpec((n_keys, WIDE), whole),
            ],
        ),
        out_shape=[
            jax.ShapeDtypeStruct((tok, heads * VDIM), BF16),
            jax.ShapeDtypeStruct((tok, heads * QDIM), BF16),
            jax.ShapeDtypeStruct((8, count, 64, LATENT), BF16),
            jax.ShapeDtypeStruct((8, count, 64, LATENT), BF16),
            jax.ShapeDtypeStruct((n_keys, WIDE), F32),
        ],
        compiler_params=pltpu.CompilerParams(vmem_limit_bytes=56 * 1024 * 1024),
        cost_estimate=pl.CostEstimate(
            flops=heads * 1_100_000_000, bytes_accessed=heads * 1_000_000, transcendentals=0
        ),
        name="attend",
    )(core, keys, bias, queries, grad_out, kv_weight)


def table_lookup(lookup_table, positions):
    hits = positions[:, None] == jnp.arange(lookup_table.shape[0], dtype=jnp.int32)[None, :]
    return jnp.sum(jnp.where(hits, lookup_table[None, :], 0), axis=1)


def shifted(shard, axis, by):
    length = lax.axis_size(axis)
    pairs = [(i, i + by) for i in range(length) if 0 <= i + by < length]
    return lax.ppermute(shard, axis, pairs)


def body(queries, compressed, kv_weight, segments, grad_out):
    scale = QDIM ** (-0.5)
    tok = queries.shape[0]
    group = lax.axis_size("inner")
    n_outer = lax.axis_size("outer")
    inner = lax.axis_index("inner")
    outer = lax.axis_index("outer")
    own_block = outer * group + inner
    core = lax.rem(outer, 2)
    slots = jnp.arange(group, dtype=jnp.int32)
    earlier = shifted(compressed, "outer", 1)
    outgoing = jnp.where((slots >= inner)[:, None, None], compressed[None], earlier[None])
    gathered = lax.all_to_all(outgoing, "inner", split_axis=0, concat_axis=0, tiled=True)
    keys = gathered.reshape(group * tok, WIDE)
    key_block = jnp.where(slots <= inner, outer * group + slots, (outer - 1) * group + slots)
    seg_keys = table_lookup(segments, key_block)
    seg_query = table_lookup(segments, own_block[None])
    slot_ok = (seg_keys == seg_query) & (key_block >= 0)
    at = jnp.arange(tok, dtype=jnp.int32)
    allowed = slot_ok[None, :, None] & (
        (slots != inner)[None, :, None] | (at[None, None, :] <= at[:, None, None])
    )
    bias = jnp.where(allowed, 0.0, -1e30).astype(F32).reshape(tok, group * tok)

    swap = [(o, o ^ 1) for o in range(n_outer)]
    attended, grad_query, dkeys, reduced = [], [], [], []
    for first, count in CHUNKS:
        att, gq, keep, send, dk = attend_chunk(
            core[None], keys, bias, queries, grad_out, kv_weight, first, count, scale
        )
        attended.append(att)
        grad_query.append(gq)
        dkeys.append(dk)
        other = lax.ppermute(send, "outer", swap)
        pair = (keep.astype(F32) + other.astype(F32)).astype(BF16)
        parts = lax.all_to_all(pair, "inner", split_axis=0, concat_axis=0, tiled=True)
        reduced.append(jnp.sum(parts.astype(F32), axis=0).astype(BF16))
    dkeys = sum(dkeys[1:], dkeys[0]).astype(BF16).reshape(group, tok, WIDE)
    arrived = lax.all_to_all(dkeys, "inner", split_axis=0, concat_axis=0, tiled=True).astype(F32)
    from_group = (slots >= inner)[:, None, None]
    own_term = jnp.sum(jnp.where(from_group, arrived, 0.0), axis=0)
    later_term = jnp.sum(jnp.where(from_group, 0.0, arrived), axis=0)
    next_term = shifted(later_term.astype(BF16), "outer", -1).astype(F32)
    grad_compressed = (own_term + next_term).astype(BF16)

    same_core = [[o for o in range(n_outer) if o % 2 == c] for c in range(2)]
    reduced = jnp.concatenate(reduced, axis=0)
    last = lax.all_to_all(
        reduced, "outer", split_axis=0, concat_axis=0, axis_index_groups=same_core, tiled=True
    )
    grad_weight_t = jnp.sum(last.astype(F32), axis=0)
    attended = jnp.concatenate(attended, axis=1)
    grad_query = jnp.concatenate(grad_query, axis=1)
    return attended, grad_query, grad_compressed, grad_weight_t


def solution(mesh):
    return jax.shard_map(
        body,
        mesh=mesh,
        in_specs=(
            P(("outer", "inner"), None),
            P(("outer", "inner"), None),
            P(),
            P(),
            P(("outer", "inner"), None),
        ),
        out_specs=(
            P(("outer", "inner"), None),
            P(("outer", "inner"), None),
            P(("outer", "inner"), None),
            P(("outer", "inner"), None),
        ),
        check_vma=False,
    )
```

```python
import functools

import jax
import jax.numpy as jnp
from jax import lax
from jax.experimental import pallas as pl
from jax.experimental.pallas import tpu as pltpu
from jax.sharding import PartitionSpec as P

LATENT = 512
NOPE = 128
ROPE = 64
VDIM = 128
HEADS = 32
TILE = 128
QDIM = NOPE + ROPE
KVDIM = NOPE + VDIM
WIDE = LATENT + ROPE
STEP_HEADS = 4
CHUNKS = ((0, 4), (4, 4))
BF16 = jnp.bfloat16
F32 = jnp.float32

ROWS_ROWS = (((1,), (1,)), ((), ()))
COLS_COLS = (((0,), (0,)), ((), ()))


def dot(a, b):
    return jnp.dot(a, b, preferred_element_type=F32)


def dot_general(a, b, dims):
    return lax.dot_general(a, b, dims, preferred_element_type=F32)


def attend_kernel(core_ref, keys_ref, bias_ref, q_ref, g_ref, w_ref, *rest, scale, is_first, is_last):
    att_ref, gq_ref, keep_ref, send_ref, dkeys_ref = rest[-6:-1]
    acc_ref = rest[-1]
    tok = q_ref.shape[0]
    keys = keys_ref[...]
    latent = keys_ref[:, :LATENT]
    q_nope, q_cat, g_heads, g_abs = [], [], [], []
    for h in range(STEP_HEADS):
        qn = q_ref[:, h * QDIM:h * QDIM + NOPE]
        qr = q_ref[:, h * QDIM + NOPE:(h + 1) * QDIM]
        g = g_ref[:, h * VDIM:(h + 1) * VDIM]
        wk = w_ref[:, h * KVDIM:h * KVDIM + NOPE]
        wv = w_ref[:, h * KVDIM + NOPE:(h + 1) * KVDIM]
        qa = (dot_general(qn, wk, ROWS_ROWS) * scale).astype(BF16)
        qr = (qr.astype(F32) * scale).astype(BF16)
        q_nope.append(qn)
        q_cat.append(jnp.concatenate([qa, qr], axis=1))
        g_heads.append(g)
        g_abs.append(dot_general(g, wv, ROWS_ROWS).astype(BF16))
    q_cat = jnp.concatenate(q_cat, axis=0)
    g_abs = jnp.concatenate(g_abs, axis=0)
    scores = dot_general(q_cat, keys, ROWS_ROWS)
    grad_probs = dot_general(g_abs, latent, ROWS_ROWS)
    bias = bias_ref[...]
    probs_half, grad_scores = [], []
    for h in range(STEP_HEADS):
        s = scores[h * tok:(h + 1) * tok] + bias
        s = jnp.exp(s - jnp.max(s, axis=1, keepdims=True))
        p = s * (1.0 / jnp.sum(s, axis=1, keepdims=True))
        gp = grad_probs[h * tok:(h + 1) * tok]
        row_dot = jnp.sum(p * gp, axis=1, keepdims=True)
        probs_half.append(p.astype(BF16))
        grad_scores.append((p * (gp - row_dot)).astype(BF16))
    probs_half = jnp.concatenate(probs_half, axis=0)
    grad_scores = jnp.concatenate(grad_scores, axis=0)

    @pl.when(pl.program_id(0) == 0)
    def _():
        acc_ref[...] = jnp.zeros_like(acc_ref) if is_first else rest[0][...]

    acc_ref[:LATENT] += dot_general(q_cat[:, :LATENT], grad_scores, COLS_COLS) + dot_general(
        g_abs, probs_half, COLS_COLS
    )
    acc_ref[LATENT:] += dot_general(q_cat[:, LATENT:], grad_scores, COLS_COLS)
    mixed = dot(probs_half, latent).astype(BF16)
    grad_mixed = dot(grad_scores, keys) * scale
    grad_mixed_lat = grad_mixed[:, :LATENT].astype(BF16)
    grad_rope = grad_mixed[:, LATENT:].astype(BF16)
    terms = []
    for h in range(STEP_HEADS):
        rows = slice(h * tok, (h + 1) * tok)
        wk = w_ref[:, h * KVDIM:h * KVDIM + NOPE]
        wv = w_ref[:, h * KVDIM + NOPE:(h + 1) * KVDIM]
        att_ref[:, h * VDIM:(h + 1) * VDIM] = dot(mixed[rows], wv).astype(BF16)
        gq_ref[:, h * QDIM:h * QDIM + NOPE] = dot(grad_mixed_lat[rows], wk).astype(BF16)
        gq_ref[:, h * QDIM + NOPE:(h + 1) * QDIM] = grad_rope[rows]
        key_term = dot_general(q_nope[h], grad_mixed_lat[rows], COLS_COLS).astype(BF16)
        value_term = dot_general(g_heads[h], mixed[rows], COLS_COLS).astype(BF16)
        terms.append((key_term, value_term))

    def put(ref, heads):
        for n, head in enumerate(heads):
            ref[n * KVDIM:n * KVDIM + NOPE] = terms[head][0]
            ref[n * KVDIM + NOPE:(n + 1) * KVDIM] = terms[head][1]

    @pl.when(core_ref[0] == 0)
    def _():
        put(keep_ref, (0, 1))
        put(send_ref, (2, 3))

    @pl.when(core_ref[0] != 0)
    def _():
        put(keep_ref, (2, 3))
        put(send_ref, (0, 1))

    @pl.when(pl.program_id(0) == pl.num_programs(0) - 1)
    def _():
        if is_last:
            dkeys_ref[...] = acc_ref[...].T.astype(BF16)
        else:
            dkeys_ref[...] = acc_ref[...]


def attend_chunk(core, keys, bias, queries, grad_out, kv_weight, held, first, count, scale):
    tok = queries.shape[0]
    n_keys = keys.shape[0]
    is_first, is_last = first == 0, (first + count) * STEP_HEADS == HEADS
    whole = lambda s, c: (0, 0)
    column = lambda s, c: (0, first + s)
    block = lambda s, c: (lax.rem(s + count - c[1], count), 0)
    heads = count * STEP_HEADS
    parts_shape = jax.ShapeDtypeStruct((count * 2 * KVDIM, LATENT), BF16)
    parts_spec = pl.BlockSpec((2 * KVDIM, LATENT), block)
    dkeys_shape = (n_keys, WIDE) if is_last else (WIDE, n_keys)
    held_specs = [
        pl.BlockSpec((WIDE, n_keys), whole),
        pl.BlockSpec(memory_space=pl.ANY),
        pl.BlockSpec(memory_space=pl.ANY),
    ]
    att, gq, keep, send, dkeys = pl.pallas_call(
        functools.partial(attend_kernel, scale=scale, is_first=is_first, is_last=is_last),
        grid_spec=pltpu.PrefetchScalarGridSpec(
            num_scalar_prefetch=1,
            grid=(count,),
            in_specs=[
                pl.BlockSpec((n_keys, WIDE), whole),
                pl.BlockSpec((tok, n_keys), whole),
                pl.BlockSpec((tok, STEP_HEADS * QDIM), column),
                pl.BlockSpec((tok, STEP_HEADS * VDIM), column),
                pl.BlockSpec((LATENT, STEP_HEADS * KVDIM), column),
            ] + held_specs[:len(held)],
            out_specs=[
                pl.BlockSpec((tok, STEP_HEADS * VDIM), column),
                pl.BlockSpec((tok, STEP_HEADS * QDIM), column),
                parts_spec,
                parts_spec,
                pl.BlockSpec(dkeys_shape, whole),
            ],
            scratch_shapes=[pltpu.VMEM((WIDE, n_keys), F32)],
        ),
        out_shape=[
            jax.ShapeDtypeStruct((tok, HEADS * VDIM), BF16),
            jax.ShapeDtypeStruct((tok, HEADS * QDIM), BF16),
            parts_shape,
            parts_shape,
            jax.ShapeDtypeStruct(dkeys_shape, BF16 if is_last else F32),
        ],
        input_output_aliases={7: 0, 8: 1} if held else {},
        compiler_params=pltpu.CompilerParams(vmem_limit_bytes=56 * 1024 * 1024),
        cost_estimate=pl.CostEstimate(
            flops=heads * 1_000_000_000, bytes_accessed=heads * 1_000_000, transcendentals=0
        ),
        name="attend",
    )(core, keys, bias, queries, grad_out, kv_weight, *held)
    return (dkeys, att, gq), keep, send


def table_lookup(lookup_table, positions):
    hits = positions[:, None] == jnp.arange(lookup_table.shape[0], dtype=jnp.int32)[None, :]
    return jnp.sum(jnp.where(hits, lookup_table[None, :], 0), axis=1)


def shifted(shard, axis, by):
    length = lax.axis_size(axis)
    pairs = [(i, i + by) for i in range(length) if 0 <= i + by < length]
    return lax.ppermute(shard, axis, pairs)


def body(queries, compressed, kv_weight, segments, grad_out):
    scale = QDIM ** (-0.5)
    tok = queries.shape[0]
    group = lax.axis_size("inner")
    n_outer = lax.axis_size("outer")
    inner = lax.axis_index("inner")
    outer = lax.axis_index("outer")
    own_block = outer * group + inner
    core = lax.rem(outer, 2)
    slots = jnp.arange(group, dtype=jnp.int32)
    earlier = shifted(compressed, "outer", 1)
    outgoing = jnp.where((slots >= inner)[:, None, None], compressed[None], earlier[None])
    gathered = lax.all_to_all(outgoing, "inner", split_axis=0, concat_axis=0, tiled=True)
    keys = gathered.reshape(group * tok, WIDE)
    key_block = jnp.where(slots <= inner, outer * group + slots, (outer - 1) * group + slots)
    seg_keys = table_lookup(segments, key_block)
    seg_query = table_lookup(segments, own_block[None])
    slot_ok = (seg_keys == seg_query) & (key_block >= 0)
    at = jnp.arange(tok, dtype=jnp.int32)
    allowed = slot_ok[None, :, None] & (
        (slots != inner)[None, :, None] | (at[None, None, :] <= at[:, None, None])
    )
    bias = jnp.where(allowed, 0.0, -1e30).astype(F32).reshape(tok, group * tok)

    swap = [(o, o ^ 1) for o in range(n_outer)]
    row_y = lax.rem(lax.div(outer, 2), 4)

    def along_y(shard, by):
        return lax.ppermute(
            shard, "outer", [(o, o // 8 * 8 + (o % 8 + 2 * by) % 8) for o in range(n_outer)]
        )

    def summed(keep, send):
        other = lax.ppermute(send, "outer", swap)
        return (keep.astype(F32) + other.astype(F32)).astype(BF16)

    which = jnp.stack([core, jnp.zeros_like(core)])
    held, keep, send = attend_chunk(
        which, keys, bias, queries, grad_out, kv_weight, (), 0, 4, scale
    )
    pair = summed(keep, send)
    which, pair = lax.optimization_barrier((jnp.stack([core, row_y]), pair))
    same_xc = [[x * 8 + y * 2 + c for y in range(4)] for x in range(2) for c in range(2)]
    first = lax.all_to_all(
        pair.reshape(4, 512, LATENT), "outer", split_axis=0, concat_axis=0,
        axis_index_groups=same_xc, tiled=True,
    )
    held, keep, send = attend_chunk(
        which, keys, bias, queries, grad_out, kv_weight, held, 4, 4, scale
    )
    held, keep, send, first = lax.optimization_barrier((held, keep, send, first))
    first = jnp.sum(first.astype(F32), axis=0).astype(BF16)
    dkeys, attended, grad_query = held
    pair = summed(keep, send).reshape(4, 512, LATENT)
    second = sum(along_y(pair[by], by).astype(F32) for by in range(1, 4))
    second = (second + pair[0].astype(F32)).astype(BF16)
    reduced = [first, second]
    dkeys = dkeys.reshape(group, tok, WIDE)
    arrived = lax.all_to_all(dkeys, "inner", split_axis=0, concat_axis=0, tiled=True).astype(F32)
    from_group = (slots >= inner)[:, None, None]
    own_term = jnp.sum(jnp.where(from_group, arrived, 0.0), axis=0)
    later_term = jnp.sum(jnp.where(from_group, 0.0, arrived), axis=0)
    next_term = shifted(later_term.astype(BF16), "outer", -1).astype(F32)
    grad_compressed = (own_term + next_term).astype(BF16)

    rest = [
        [(x * 8 + y * 2 + c) * group + i for x in range(2) for i in range(group)]
        for y in range(4) for c in range(2)
    ]
    reduced = jnp.concatenate(reduced, axis=0).reshape(16, 64, LATENT)
    last = lax.all_to_all(
        reduced, ("outer", "inner"), split_axis=0, concat_axis=0, axis_index_groups=rest, tiled=True
    )
    grad_weight_t = jnp.sum(last.astype(F32), axis=0)
    return attended, grad_query, grad_compressed, grad_weight_t


def solution(mesh):
    return jax.shard_map(
        body,
        mesh=mesh,
        in_specs=(
            P(("outer", "inner"), None),
            P(("outer", "inner"), None),
            P(),
            P(),
            P(("outer", "inner"), None),
        ),
        out_specs=(
            P(("outer", "inner"), None),
            P(("outer", "inner"), None),
            P(("outer", "inner"), None),
            P(("outer", "inner"), None),
        ),
        check_vma=False,
    )
```

```python
import functools

import jax
import jax.numpy as jnp
from jax import lax
from jax.experimental import pallas as pl
from jax.experimental.pallas import tpu as pltpu
from jax.sharding import PartitionSpec as P

LATENT = 512
NOPE = 128
ROPE = 64
VDIM = 128
HEADS = 32
TILE = 128
QDIM = NOPE + ROPE
KVDIM = NOPE + VDIM
WIDE = LATENT + ROPE
STEP_HEADS = 4
CHUNKS = ((0, 4), (4, 4))
BF16 = jnp.bfloat16
F32 = jnp.float32

ROWS_ROWS = (((1,), (1,)), ((), ()))
COLS_COLS = (((0,), (0,)), ((), ()))


def dot(a, b):
    return jnp.dot(a, b, preferred_element_type=F32)


def dot_general(a, b, dims):
    return lax.dot_general(a, b, dims, preferred_element_type=F32)


def attend_kernel(core_ref, keys_ref, bias_ref, q_ref, g_ref, w_ref, *rest, scale, is_first, is_last):
    att_ref, gq_ref, keep_ref, send_ref, dkeys_ref, keys_t_ref, *acc = rest if is_first else rest[3:]
    acc_ref = acc[0] if is_last else dkeys_ref
    tok = q_ref.shape[0]
    slots = keys_ref.shape[0]

    @pl.when(pl.program_id(0) == 0)
    def _():
        acc_ref[...] = jnp.zeros_like(acc_ref) if is_first else rest[0][...]
        for s in range(slots):
            keys_t_ref[:, s * tok:(s + 1) * tok] = keys_ref[s]

    def q_nope(h):
        return q_ref[:, h * QDIM:h * QDIM + NOPE]

    def grad_head(h):
        return g_ref[:, h * VDIM:(h + 1) * VDIM]

    def key_weight(h):
        return w_ref[:, h * KVDIM:h * KVDIM + NOPE]

    def value_weight(h):
        return w_ref[:, h * KVDIM + NOPE:(h + 1) * KVDIM]

    keys_t = keys_t_ref[...]
    latent_t = keys_t_ref[:LATENT]
    q_cat, g_abs = [], []
    for h in range(STEP_HEADS):
        qa = (dot_general(q_nope(h), key_weight(h), ROWS_ROWS) * scale).astype(BF16)
        qr = (q_ref[:, h * QDIM + NOPE:(h + 1) * QDIM].astype(F32) * scale).astype(BF16)
        q_cat.append(jnp.concatenate([qa, qr], axis=1))
        g_abs.append(dot_general(grad_head(h), value_weight(h), ROWS_ROWS).astype(BF16))
    q_cat = jnp.concatenate(q_cat, axis=0)
    g_abs = jnp.concatenate(g_abs, axis=0)
    scores = dot(q_cat, keys_t)
    grad_probs = dot(g_abs, latent_t)
    bias = bias_ref[...]
    probs_half, grad_scores = [], []
    for h in range(STEP_HEADS):
        s = scores[h * tok:(h + 1) * tok] + bias
        s = jnp.exp(s - jnp.max(s, axis=1, keepdims=True))
        p = s * (1.0 / jnp.sum(s, axis=1, keepdims=True))
        gp = grad_probs[h * tok:(h + 1) * tok]
        row_dot = jnp.sum(p * gp, axis=1, keepdims=True)
        probs_half.append(p.astype(BF16))
        grad_scores.append((p * (gp - row_dot)).astype(BF16))
    probs_half = jnp.concatenate(probs_half, axis=0)
    grad_scores = jnp.concatenate(grad_scores, axis=0)
    acc_ref[:LATENT] += dot_general(q_cat[:, :LATENT], grad_scores, COLS_COLS) + dot_general(
        g_abs, probs_half, COLS_COLS
    )
    acc_ref[LATENT:] += dot_general(q_cat[:, LATENT:], grad_scores, COLS_COLS)
    mixed = dot_general(probs_half, latent_t, ROWS_ROWS).astype(BF16)
    grad_mixed = dot_general(grad_scores, keys_t, ROWS_ROWS) * scale
    grad_mixed_lat = grad_mixed[:, :LATENT].astype(BF16)
    grad_rope = grad_mixed[:, LATENT:].astype(BF16)
    terms = []
    for h in range(STEP_HEADS):
        rows = slice(h * tok, (h + 1) * tok)
        att_ref[:, h * VDIM:(h + 1) * VDIM] = dot(mixed[rows], value_weight(h)).astype(BF16)
        gq_ref[:, h * QDIM:h * QDIM + NOPE] = dot(grad_mixed_lat[rows], key_weight(h)).astype(BF16)
        gq_ref[:, h * QDIM + NOPE:(h + 1) * QDIM] = grad_rope[rows]
        key_term = dot_general(q_nope(h), grad_mixed_lat[rows], COLS_COLS).astype(BF16)
        value_term = dot_general(grad_head(h), mixed[rows], COLS_COLS).astype(BF16)
        terms.append((key_term, value_term))

    def put(ref, heads):
        for n, head in enumerate(heads):
            ref[n * KVDIM:n * KVDIM + NOPE] = terms[head][0]
            ref[n * KVDIM + NOPE:(n + 1) * KVDIM] = terms[head][1]

    @pl.when(core_ref[0] == 0)
    def _():
        put(keep_ref, (0, 1))
        put(send_ref, (2, 3))

    @pl.when(core_ref[0] != 0)
    def _():
        put(keep_ref, (2, 3))
        put(send_ref, (0, 1))

    if is_last:
        @pl.when(pl.program_id(0) == pl.num_programs(0) - 1)
        def _():
            for s in range(slots):
                dkeys_ref[s] = acc_ref[:, s * tok:(s + 1) * tok].astype(BF16)


def attend_chunk(core, keys, bias, queries, grad_out, kv_weight, held, first, count, scale):
    tok = queries.shape[0]
    slots = keys.shape[0]
    n_keys = slots * tok
    is_first, is_last = first == 0, (first + count) * STEP_HEADS == HEADS
    whole = lambda s, c: (0, 0)
    column = lambda s, c: (0, first + s)
    block = lambda s, c: (lax.rem(s + count - c[1], count), 0)
    heads = count * STEP_HEADS
    parts_shape = jax.ShapeDtypeStruct((count * 2 * KVDIM, LATENT), BF16)
    parts_spec = pl.BlockSpec((2 * KVDIM, LATENT), block)
    dkeys_shape = keys.shape if is_last else (WIDE, n_keys)
    whole3 = lambda s, c: (0, 0, 0)
    held_specs = [
        pl.BlockSpec((WIDE, n_keys), whole),
        pl.BlockSpec(memory_space=pl.ANY),
        pl.BlockSpec(memory_space=pl.ANY),
    ]
    att, gq, keep, send, dkeys = pl.pallas_call(
        functools.partial(attend_kernel, scale=scale, is_first=is_first, is_last=is_last),
        grid_spec=pltpu.PrefetchScalarGridSpec(
            num_scalar_prefetch=1,
            grid=(count,),
            in_specs=[
                pl.BlockSpec(keys.shape, whole3),
                pl.BlockSpec((tok, n_keys), whole),
                pl.BlockSpec((tok, STEP_HEADS * QDIM), column),
                pl.BlockSpec((tok, STEP_HEADS * VDIM), column),
                pl.BlockSpec((LATENT, STEP_HEADS * KVDIM), column),
            ] + held_specs[:len(held)],
            out_specs=[
                pl.BlockSpec((tok, STEP_HEADS * VDIM), column),
                pl.BlockSpec((tok, STEP_HEADS * QDIM), column),
                parts_spec,
                parts_spec,
                pl.BlockSpec(dkeys_shape, whole3 if is_last else whole),
            ],
            scratch_shapes=[pltpu.VMEM((WIDE, n_keys), BF16)]
            + [pltpu.VMEM((WIDE, n_keys), F32)] * is_last,
        ),
        out_shape=[
            jax.ShapeDtypeStruct((tok, HEADS * VDIM), BF16),
            jax.ShapeDtypeStruct((tok, HEADS * QDIM), BF16),
            parts_shape,
            parts_shape,
            jax.ShapeDtypeStruct(dkeys_shape, BF16 if is_last else F32),
        ],
        input_output_aliases={7: 0, 8: 1} if held else {},
        compiler_params=pltpu.CompilerParams(vmem_limit_bytes=56 * 1024 * 1024),
        cost_estimate=pl.CostEstimate(
            flops=heads * 1_000_000_000, bytes_accessed=heads * 1_000_000, transcendentals=0
        ),
        name="attend",
    )(core, keys, bias, queries, grad_out, kv_weight, *held)
    return (dkeys, att, gq), keep, send


def table_lookup(lookup_table, positions):
    hits = positions[:, None] == jnp.arange(lookup_table.shape[0], dtype=jnp.int32)[None, :]
    return jnp.sum(jnp.where(hits, lookup_table[None, :], 0), axis=1)


def shifted(shard, axis, by):
    length = lax.axis_size(axis)
    pairs = [(i, i + by) for i in range(length) if 0 <= i + by < length]
    return lax.ppermute(shard, axis, pairs)


def body(queries, compressed, kv_weight, segments, grad_out):
    scale = QDIM ** (-0.5)
    tok = queries.shape[0]
    group = lax.axis_size("inner")
    n_outer = lax.axis_size("outer")
    inner = lax.axis_index("inner")
    outer = lax.axis_index("outer")
    own_block = outer * group + inner
    core = lax.rem(outer, 2)
    slots = jnp.arange(group, dtype=jnp.int32)
    own = compressed.T
    earlier = shifted(own, "outer", 1)
    outgoing = jnp.where((slots >= inner)[:, None, None], own[None], earlier[None])
    keys = lax.all_to_all(outgoing, "inner", split_axis=0, concat_axis=0, tiled=True)
    key_block = jnp.where(slots <= inner, outer * group + slots, (outer - 1) * group + slots)
    seg_keys = table_lookup(segments, key_block)
    seg_query = table_lookup(segments, own_block[None])
    slot_ok = (seg_keys == seg_query) & (key_block >= 0)
    at = jnp.arange(tok, dtype=jnp.int32)
    allowed = slot_ok[None, :, None] & (
        (slots != inner)[None, :, None] | (at[None, None, :] <= at[:, None, None])
    )
    bias = jnp.where(allowed, 0.0, -1e30).astype(F32).reshape(tok, group * tok)

    swap = [(o, o ^ 1) for o in range(n_outer)]
    row_y = lax.rem(lax.div(outer, 2), 4)

    def along_y(shard, by):
        return lax.ppermute(
            shard, "outer", [(o, o // 8 * 8 + (o % 8 + 2 * by) % 8) for o in range(n_outer)]
        )

    def summed(keep, send):
        other = lax.ppermute(send, "outer", swap)
        return (keep.astype(F32) + other.astype(F32)).astype(BF16)

    which = jnp.stack([core, jnp.zeros_like(core)])
    held, keep, send = attend_chunk(
        which, keys, bias, queries, grad_out, kv_weight, (), 0, 4, scale
    )
    pair = summed(keep, send)
    which, pair = lax.optimization_barrier((jnp.stack([core, row_y]), pair))
    same_xc = [[x * 8 + y * 2 + c for y in range(4)] for x in range(2) for c in range(2)]
    first = lax.all_to_all(
        pair.reshape(4, 512, LATENT), "outer", split_axis=0, concat_axis=0,
        axis_index_groups=same_xc, tiled=True,
    )
    held, keep, send = attend_chunk(
        which, keys, bias, queries, grad_out, kv_weight, held, 4, 4, scale
    )
    held, keep, send, first = lax.optimization_barrier((held, keep, send, first))
    first = jnp.sum(first.astype(F32), axis=0).astype(BF16)
    dkeys, attended, grad_query = held
    pair = summed(keep, send).reshape(4, 512, LATENT)
    second = sum(along_y(pair[by], by).astype(F32) for by in range(1, 4))
    second = (second + pair[0].astype(F32)).astype(BF16)
    reduced = [first, second]
    arrived = lax.all_to_all(dkeys, "inner", split_axis=0, concat_axis=0, tiled=True).astype(F32)
    from_group = (slots >= inner)[:, None, None]
    own_term = jnp.sum(jnp.where(from_group, arrived, 0.0), axis=0)
    later_term = jnp.sum(jnp.where(from_group, 0.0, arrived), axis=0)
    next_term = shifted(later_term.astype(BF16), "outer", -1).astype(F32)
    grad_compressed = (own_term + next_term).astype(BF16).T

    rest = [
        [(x * 8 + y * 2 + c) * group + i for x in range(2) for i in range(group)]
        for y in range(4) for c in range(2)
    ]
    reduced = jnp.concatenate(reduced, axis=0).reshape(16, 64, LATENT)
    last = lax.all_to_all(
        reduced, ("outer", "inner"), split_axis=0, concat_axis=0, axis_index_groups=rest, tiled=True
    )
    grad_weight_t = jnp.sum(last.astype(F32), axis=0)
    return attended, grad_query, grad_compressed, grad_weight_t


def solution(mesh):
    return jax.shard_map(
        body,
        mesh=mesh,
        in_specs=(
            P(("outer", "inner"), None),
            P(("outer", "inner"), None),
            P(),
            P(),
            P(("outer", "inner"), None),
        ),
        out_specs=(
            P(("outer", "inner"), None),
            P(("outer", "inner"), None),
            P(("outer", "inner"), None),
            P(("outer", "inner"), None),
        ),
        check_vma=False,
    )
```

```python
import functools

import jax
import jax.numpy as jnp
from jax import lax
from jax.experimental import pallas as pl
from jax.experimental.pallas import tpu as pltpu
from jax.sharding import PartitionSpec as P

LATENT = 512
NOPE = 128
ROPE = 64
VDIM = 128
HEADS = 32
TILE = 128
QDIM = NOPE + ROPE
KVDIM = NOPE + VDIM
WIDE = LATENT + ROPE
STEP_HEADS = 4
CHUNKS = ((0, 4), (4, 4))
BF16 = jnp.bfloat16
F32 = jnp.float32

ROWS_ROWS = (((1,), (1,)), ((), ()))
COLS_COLS = (((0,), (0,)), ((), ()))


def dot(a, b):
    return jnp.dot(a, b, preferred_element_type=F32)


def dot_general(a, b, dims):
    return lax.dot_general(a, b, dims, preferred_element_type=F32)


def absorb_kernel(q_ref, g_ref, w_ref, qc_ref, ga_ref, *, scale):
    tok = q_ref.shape[0]
    for h in range(STEP_HEADS):
        rows = slice(h * tok, (h + 1) * tok)
        q_nope = q_ref[:, h * QDIM:h * QDIM + NOPE]
        q_rope = q_ref[:, h * QDIM + NOPE:(h + 1) * QDIM]
        key_weight = w_ref[:, h * KVDIM:h * KVDIM + NOPE]
        value_weight = w_ref[:, h * KVDIM + NOPE:(h + 1) * KVDIM]
        qc_ref[rows, :LATENT] = (dot_general(q_nope, key_weight, ROWS_ROWS) * scale).astype(BF16)
        qc_ref[rows, LATENT:] = (q_rope.astype(F32) * scale).astype(BF16)
        grad_head = g_ref[:, h * VDIM:(h + 1) * VDIM]
        ga_ref[rows] = dot_general(grad_head, value_weight, ROWS_ROWS).astype(BF16)


def absorb(queries, grad_out, kv_weight, scale):
    tok = queries.shape[0]
    rows = STEP_HEADS * tok
    column = lambda s: (0, s)
    row = lambda s: (s, 0)
    return pl.pallas_call(
        functools.partial(absorb_kernel, scale=scale),
        grid=(HEADS // STEP_HEADS,),
        in_specs=[
            pl.BlockSpec((tok, STEP_HEADS * QDIM), column),
            pl.BlockSpec((tok, STEP_HEADS * VDIM), column),
            pl.BlockSpec((LATENT, STEP_HEADS * KVDIM), column),
        ],
        out_specs=[pl.BlockSpec((rows, WIDE), row), pl.BlockSpec((rows, LATENT), row)],
        out_shape=[
            jax.ShapeDtypeStruct((HEADS * tok, WIDE), BF16),
            jax.ShapeDtypeStruct((HEADS * tok, LATENT), BF16),
        ],
        compiler_params=pltpu.CompilerParams(vmem_limit_bytes=24 * 1024 * 1024),
        cost_estimate=pl.CostEstimate(
            flops=6_000_000_000, bytes_accessed=20_000_000, transcendentals=0
        ),
        name="absorb",
    )(queries, grad_out, kv_weight)


def attend_kernel(core_ref, keys_ref, bias_ref, qc_ref, ga_ref, q_ref, g_ref, w_ref, *rest, scale, is_first, is_last):
    att_ref, gq_ref, keep_ref, send_ref, dkeys_ref, keys_t_ref, *acc = rest if is_first else rest[3:]
    acc_ref = acc[0] if is_last else dkeys_ref
    tok = q_ref.shape[0]
    slots = keys_ref.shape[0]

    @pl.when(pl.program_id(0) == 0)
    def _():
        acc_ref[...] = jnp.zeros_like(acc_ref) if is_first else rest[0][...]
        for s in range(slots):
            keys_t_ref[:, s * tok:(s + 1) * tok] = keys_ref[s]

    def q_nope(h):
        return q_ref[:, h * QDIM:h * QDIM + NOPE]

    def grad_head(h):
        return g_ref[:, h * VDIM:(h + 1) * VDIM]

    def key_weight(h):
        return w_ref[:, h * KVDIM:h * KVDIM + NOPE]

    def value_weight(h):
        return w_ref[:, h * KVDIM + NOPE:(h + 1) * KVDIM]

    keys_t = keys_t_ref[...]
    latent_t = keys_t_ref[:LATENT]
    q_cat = qc_ref[...]
    g_abs = ga_ref[...]
    scores = dot(q_cat, keys_t)
    grad_probs = dot(g_abs, latent_t)
    bias = bias_ref[...]
    probs_half, grad_scores = [], []
    for h in range(STEP_HEADS):
        s = scores[h * tok:(h + 1) * tok] + bias
        s = jnp.exp(s - jnp.max(s, axis=1, keepdims=True))
        p = s * (1.0 / jnp.sum(s, axis=1, keepdims=True))
        gp = grad_probs[h * tok:(h + 1) * tok]
        row_dot = jnp.sum(p * gp, axis=1, keepdims=True)
        probs_half.append(p.astype(BF16))
        grad_scores.append((p * (gp - row_dot)).astype(BF16))
    probs_half = jnp.concatenate(probs_half, axis=0)
    grad_scores = jnp.concatenate(grad_scores, axis=0)
    acc_ref[:LATENT] += dot_general(q_cat[:, :LATENT], grad_scores, COLS_COLS) + dot_general(
        g_abs, probs_half, COLS_COLS
    )
    acc_ref[LATENT:] += dot_general(q_cat[:, LATENT:], grad_scores, COLS_COLS)
    mixed = dot_general(probs_half, latent_t, ROWS_ROWS).astype(BF16)
    grad_mixed = dot_general(grad_scores, keys_t, ROWS_ROWS) * scale
    grad_mixed_lat = grad_mixed[:, :LATENT].astype(BF16)
    grad_rope = grad_mixed[:, LATENT:].astype(BF16)
    terms = []
    for h in range(STEP_HEADS):
        rows = slice(h * tok, (h + 1) * tok)
        att_ref[:, h * VDIM:(h + 1) * VDIM] = dot(mixed[rows], value_weight(h)).astype(BF16)
        gq_ref[:, h * QDIM:h * QDIM + NOPE] = dot(grad_mixed_lat[rows], key_weight(h)).astype(BF16)
        gq_ref[:, h * QDIM + NOPE:(h + 1) * QDIM] = grad_rope[rows]
        key_term = dot_general(q_nope(h), grad_mixed_lat[rows], COLS_COLS).astype(BF16)
        value_term = dot_general(grad_head(h), mixed[rows], COLS_COLS).astype(BF16)
        terms.append((key_term, value_term))

    def put(ref, heads):
        for n, head in enumerate(heads):
            ref[n * KVDIM:n * KVDIM + NOPE] = terms[head][0]
            ref[n * KVDIM + NOPE:(n + 1) * KVDIM] = terms[head][1]

    @pl.when(core_ref[0] == 0)
    def _():
        put(keep_ref, (0, 1))
        put(send_ref, (2, 3))

    @pl.when(core_ref[0] != 0)
    def _():
        put(keep_ref, (2, 3))
        put(send_ref, (0, 1))

    if is_last:
        @pl.when(pl.program_id(0) == pl.num_programs(0) - 1)
        def _():
            for s in range(slots):
                dkeys_ref[s] = acc_ref[:, s * tok:(s + 1) * tok].astype(BF16)


def attend_chunk(core, keys, bias, absorbed, queries, grad_out, kv_weight, held, first, count, scale):
    tok = queries.shape[0]
    slots = keys.shape[0]
    n_keys = slots * tok
    is_first, is_last = first == 0, (first + count) * STEP_HEADS == HEADS
    whole = lambda s, c: (0, 0)
    column = lambda s, c: (0, first + s)
    row = lambda s, c: (first + s, 0)
    block = lambda s, c: (lax.rem(s + count - c[1], count), 0)
    heads = count * STEP_HEADS
    parts_shape = jax.ShapeDtypeStruct((count * 2 * KVDIM, LATENT), BF16)
    parts_spec = pl.BlockSpec((2 * KVDIM, LATENT), block)
    dkeys_shape = keys.shape if is_last else (WIDE, n_keys)
    whole3 = lambda s, c: (0, 0, 0)
    held_specs = [
        pl.BlockSpec((WIDE, n_keys), whole),
        pl.BlockSpec(memory_space=pl.ANY),
        pl.BlockSpec(memory_space=pl.ANY),
    ]
    att, gq, keep, send, dkeys = pl.pallas_call(
        functools.partial(attend_kernel, scale=scale, is_first=is_first, is_last=is_last),
        grid_spec=pltpu.PrefetchScalarGridSpec(
            num_scalar_prefetch=1,
            grid=(count,),
            in_specs=[
                pl.BlockSpec(keys.shape, whole3),
                pl.BlockSpec((tok, n_keys), whole),
                pl.BlockSpec((STEP_HEADS * tok, WIDE), row),
                pl.BlockSpec((STEP_HEADS * tok, LATENT), row),
                pl.BlockSpec((tok, STEP_HEADS * QDIM), column),
                pl.BlockSpec((tok, STEP_HEADS * VDIM), column),
                pl.BlockSpec((LATENT, STEP_HEADS * KVDIM), column),
            ] + held_specs[:len(held)],
            out_specs=[
                pl.BlockSpec((tok, STEP_HEADS * VDIM), column),
                pl.BlockSpec((tok, STEP_HEADS * QDIM), column),
                parts_spec,
                parts_spec,
                pl.BlockSpec(dkeys_shape, whole3 if is_last else whole),
            ],
            scratch_shapes=[pltpu.VMEM((WIDE, n_keys), BF16)]
            + [pltpu.VMEM((WIDE, n_keys), F32)] * is_last,
        ),
        out_shape=[
            jax.ShapeDtypeStruct((tok, HEADS * VDIM), BF16),
            jax.ShapeDtypeStruct((tok, HEADS * QDIM), BF16),
            parts_shape,
            parts_shape,
            jax.ShapeDtypeStruct(dkeys_shape, BF16 if is_last else F32),
        ],
        input_output_aliases={9: 0, 10: 1} if held else {},
        compiler_params=pltpu.CompilerParams(vmem_limit_bytes=56 * 1024 * 1024),
        cost_estimate=pl.CostEstimate(
            flops=heads * 1_000_000_000, bytes_accessed=heads * 1_000_000, transcendentals=0
        ),
        name="attend",
    )(core, keys, bias, *absorbed, queries, grad_out, kv_weight, *held)
    return (dkeys, att, gq), keep, send


def table_lookup(lookup_table, positions):
    hits = positions[:, None] == jnp.arange(lookup_table.shape[0], dtype=jnp.int32)[None, :]
    return jnp.sum(jnp.where(hits, lookup_table[None, :], 0), axis=1)


def shifted(shard, axis, by):
    length = lax.axis_size(axis)
    pairs = [(i, i + by) for i in range(length) if 0 <= i + by < length]
    return lax.ppermute(shard, axis, pairs)


def body(queries, compressed, kv_weight, segments, grad_out):
    scale = QDIM ** (-0.5)
    tok = queries.shape[0]
    group = lax.axis_size("inner")
    n_outer = lax.axis_size("outer")
    inner = lax.axis_index("inner")
    outer = lax.axis_index("outer")
    own_block = outer * group + inner
    core = lax.rem(outer, 2)
    slots = jnp.arange(group, dtype=jnp.int32)
    own = compressed.T
    earlier = shifted(own, "outer", 1)
    outgoing = jnp.where((slots >= inner)[:, None, None], own[None], earlier[None])
    keys = lax.all_to_all(outgoing, "inner", split_axis=0, concat_axis=0, tiled=True)
    key_block = jnp.where(slots <= inner, outer * group + slots, (outer - 1) * group + slots)
    seg_keys = table_lookup(segments, key_block)
    seg_query = table_lookup(segments, own_block[None])
    slot_ok = (seg_keys == seg_query) & (key_block >= 0)
    at = jnp.arange(tok, dtype=jnp.int32)
    allowed = slot_ok[None, :, None] & (
        (slots != inner)[None, :, None] | (at[None, None, :] <= at[:, None, None])
    )
    bias = jnp.where(allowed, 0.0, -1e30).astype(F32).reshape(tok, group * tok)

    swap = [(o, o ^ 1) for o in range(n_outer)]
    row_y = lax.rem(lax.div(outer, 2), 4)

    def along_y(shard, by):
        return lax.ppermute(
            shard, "outer", [(o, o // 8 * 8 + (o % 8 + 2 * by) % 8) for o in range(n_outer)]
        )

    def summed(keep, send):
        other = lax.ppermute(send, "outer", swap)
        return (keep.astype(F32) + other.astype(F32)).astype(BF16)

    absorbed = absorb(queries, grad_out, kv_weight, scale)
    which = jnp.stack([core, jnp.zeros_like(core)])
    held, keep, send = attend_chunk(
        which, keys, bias, absorbed, queries, grad_out, kv_weight, (), 0, 4, scale
    )
    pair = summed(keep, send)
    which, pair = lax.optimization_barrier((jnp.stack([core, row_y]), pair))
    same_xc = [[x * 8 + y * 2 + c for y in range(4)] for x in range(2) for c in range(2)]
    first = lax.all_to_all(
        pair.reshape(4, 512, LATENT), "outer", split_axis=0, concat_axis=0,
        axis_index_groups=same_xc, tiled=True,
    )
    held, keep, send = attend_chunk(
        which, keys, bias, absorbed, queries, grad_out, kv_weight, held, 4, 4, scale
    )
    held, keep, send, first = lax.optimization_barrier((held, keep, send, first))
    dkeys, attended, grad_query = held
    other = lax.ppermute(send, "outer", swap)

    def piece(by):
        rows = slice(by * 512, (by + 1) * 512)
        return (keep[rows].astype(F32) + other[rows].astype(F32)).astype(BF16)

    moved = [along_y(piece(by), by) for by in (2, 1, 3)]
    arrived = lax.all_to_all(dkeys, "inner", split_axis=0, concat_axis=0, tiled=True)
    own_piece, first, arrived = lax.optimization_barrier((piece(0), first, arrived))
    second = sum(m.astype(F32) for m in moved) + own_piece.astype(F32)

    def along_inner(part):
        part = part.astype(BF16).reshape(group, 64, LATENT)
        part = lax.all_to_all(part, "inner", split_axis=0, concat_axis=0, tiled=True)
        return jnp.sum(part.astype(F32), axis=0)

    arrived = arrived.astype(F32)
    from_group = (slots >= inner)[:, None, None]
    own_term = jnp.sum(jnp.where(from_group, arrived, 0.0), axis=0)
    later_term = jnp.sum(jnp.where(from_group, 0.0, arrived), axis=0)
    next_term = shifted(later_term.astype(BF16), "outer", -1).astype(F32)
    grad_compressed = (own_term + next_term).astype(BF16).T

    first = along_inner(jnp.sum(first.astype(F32), axis=0))
    second = along_inner(second)
    low = outer < 8
    crossing = jnp.where(low, second, first).astype(BF16)
    crossing = lax.ppermute(crossing, "outer", [(o, o ^ 8) for o in range(n_outer)])
    grad_weight_t = jnp.where(low, first, second) + crossing.astype(F32)
    return attended, grad_query, grad_compressed, grad_weight_t


def solution(mesh):
    return jax.shard_map(
        body,
        mesh=mesh,
        in_specs=(
            P(("outer", "inner"), None),
            P(("outer", "inner"), None),
            P(),
            P(),
            P(("outer", "inner"), None),
        ),
        out_specs=(
            P(("outer", "inner"), None),
            P(("outer", "inner"), None),
            P(("outer", "inner"), None),
            P(("outer", "inner"), None),
        ),
        check_vma=False,
    )
```

```python
import functools

import jax
import jax.numpy as jnp
from jax import lax
from jax.experimental import pallas as pl
from jax.experimental.pallas import tpu as pltpu
from jax.sharding import PartitionSpec as P

LATENT = 512
NOPE = 128
ROPE = 64
VDIM = 128
HEADS = 32
TILE = 128
QDIM = NOPE + ROPE
KVDIM = NOPE + VDIM
WIDE = LATENT + ROPE
STEP_HEADS = 4
CHUNKS = ((0, 4), (4, 4))
BF16 = jnp.bfloat16
F32 = jnp.float32

ROWS_ROWS = (((1,), (1,)), ((), ()))
COLS_COLS = (((0,), (0,)), ((), ()))


def dot(a, b):
    return jnp.dot(a, b, preferred_element_type=F32)


def dot_general(a, b, dims):
    return lax.dot_general(a, b, dims, preferred_element_type=F32)


def absorb_kernel(q_ref, g_ref, w_ref, qc_ref, ga_ref, *, scale):
    tok = q_ref.shape[0]
    for h in range(STEP_HEADS):
        rows = slice(h * tok, (h + 1) * tok)
        q_nope = q_ref[:, h * QDIM:h * QDIM + NOPE]
        q_rope = q_ref[:, h * QDIM + NOPE:(h + 1) * QDIM]
        key_weight = w_ref[:, h * KVDIM:h * KVDIM + NOPE]
        value_weight = w_ref[:, h * KVDIM + NOPE:(h + 1) * KVDIM]
        qc_ref[rows, :LATENT] = (dot_general(q_nope, key_weight, ROWS_ROWS) * scale).astype(BF16)
        qc_ref[rows, LATENT:] = (q_rope.astype(F32) * scale).astype(BF16)
        grad_head = g_ref[:, h * VDIM:(h + 1) * VDIM]
        ga_ref[rows] = dot_general(grad_head, value_weight, ROWS_ROWS).astype(BF16)


def absorb(queries, grad_out, kv_weight, scale):
    tok = queries.shape[0]
    rows = STEP_HEADS * tok
    column = lambda s: (0, s)
    row = lambda s: (s, 0)
    return pl.pallas_call(
        functools.partial(absorb_kernel, scale=scale),
        grid=(HEADS // STEP_HEADS,),
        in_specs=[
            pl.BlockSpec((tok, STEP_HEADS * QDIM), column),
            pl.BlockSpec((tok, STEP_HEADS * VDIM), column),
            pl.BlockSpec((LATENT, STEP_HEADS * KVDIM), column),
        ],
        out_specs=[pl.BlockSpec((rows, WIDE), row), pl.BlockSpec((rows, LATENT), row)],
        out_shape=[
            jax.ShapeDtypeStruct((HEADS * tok, WIDE), BF16),
            jax.ShapeDtypeStruct((HEADS * tok, LATENT), BF16),
        ],
        compiler_params=pltpu.CompilerParams(vmem_limit_bytes=24 * 1024 * 1024),
        cost_estimate=pl.CostEstimate(
            flops=6_000_000_000, bytes_accessed=20_000_000, transcendentals=0
        ),
        name="absorb",
    )(queries, grad_out, kv_weight)


def attend_kernel(core_ref, keys_ref, bias_ref, qc_ref, ga_ref, q_ref, g_ref, w_ref, *rest, scale, is_first, is_last):
    att_ref, gq_ref, keep_ref, send_ref, dkeys_ref, keys_t_ref, *acc = rest if is_first else rest[3:]
    acc_ref = acc[0] if is_last else dkeys_ref
    tok = q_ref.shape[0]
    slots = keys_ref.shape[0]

    @pl.when(pl.program_id(0) == 0)
    def _():
        acc_ref[...] = jnp.zeros_like(acc_ref) if is_first else rest[0][...]
        for s in range(slots):
            keys_t_ref[:, s * tok:(s + 1) * tok] = keys_ref[s]

    def q_nope(h):
        return q_ref[:, h * QDIM:h * QDIM + NOPE]

    def grad_head(h):
        return g_ref[:, h * VDIM:(h + 1) * VDIM]

    def key_weight(h):
        return w_ref[:, h * KVDIM:h * KVDIM + NOPE]

    def value_weight(h):
        return w_ref[:, h * KVDIM + NOPE:(h + 1) * KVDIM]

    keys_t = keys_t_ref[...]
    latent_t = keys_t_ref[:LATENT]
    q_cat = qc_ref[...]
    g_abs = ga_ref[...]
    scores = dot(q_cat, keys_t)
    grad_probs = dot(g_abs, latent_t)
    bias = bias_ref[...]
    probs_half, grad_scores = [], []
    for h in range(STEP_HEADS):
        s = scores[h * tok:(h + 1) * tok] + bias
        s = jnp.exp(s - jnp.max(s, axis=1, keepdims=True))
        p = s * (1.0 / jnp.sum(s, axis=1, keepdims=True))
        gp = grad_probs[h * tok:(h + 1) * tok]
        row_dot = jnp.sum(p * gp, axis=1, keepdims=True)
        probs_half.append(p.astype(BF16))
        grad_scores.append((p * (gp - row_dot)).astype(BF16))
    probs_half = jnp.concatenate(probs_half, axis=0)
    grad_scores = jnp.concatenate(grad_scores, axis=0)
    acc_ref[:LATENT] += dot_general(q_cat[:, :LATENT], grad_scores, COLS_COLS) + dot_general(
        g_abs, probs_half, COLS_COLS
    )
    acc_ref[LATENT:] += dot_general(q_cat[:, LATENT:], grad_scores, COLS_COLS)
    mixed = dot_general(probs_half, latent_t, ROWS_ROWS).astype(BF16)
    grad_mixed = dot_general(grad_scores, keys_t, ROWS_ROWS) * scale
    grad_mixed_lat = grad_mixed[:, :LATENT].astype(BF16)
    grad_rope = grad_mixed[:, LATENT:].astype(BF16)
    terms = []
    for h in range(STEP_HEADS):
        rows = slice(h * tok, (h + 1) * tok)
        att_ref[:, h * VDIM:(h + 1) * VDIM] = dot(mixed[rows], value_weight(h)).astype(BF16)
        gq_ref[:, h * QDIM:h * QDIM + NOPE] = dot(grad_mixed_lat[rows], key_weight(h)).astype(BF16)
        gq_ref[:, h * QDIM + NOPE:(h + 1) * QDIM] = grad_rope[rows]
        key_term = dot_general(q_nope(h), grad_mixed_lat[rows], COLS_COLS).astype(BF16)
        value_term = dot_general(grad_head(h), mixed[rows], COLS_COLS).astype(BF16)
        terms.append((key_term, value_term))

    def put(ref, heads):
        for n, head in enumerate(heads):
            ref[n * KVDIM:n * KVDIM + NOPE] = terms[head][0]
            ref[n * KVDIM + NOPE:(n + 1) * KVDIM] = terms[head][1]

    @pl.when(core_ref[0] == 0)
    def _():
        put(keep_ref, (0, 1))
        put(send_ref, (2, 3))

    @pl.when(core_ref[0] != 0)
    def _():
        put(keep_ref, (2, 3))
        put(send_ref, (0, 1))

    if is_last:
        @pl.when(pl.program_id(0) == pl.num_programs(0) - 1)
        def _():
            for s in range(slots):
                dkeys_ref[s] = acc_ref[:, s * tok:(s + 1) * tok].astype(BF16)


def attend_chunk(core, keys, bias, absorbed, queries, grad_out, kv_weight, held, first, count, scale):
    tok = queries.shape[0]
    slots = keys.shape[0]
    n_keys = slots * tok
    is_first, is_last = first == 0, (first + count) * STEP_HEADS == HEADS
    whole = lambda s, c: (0, 0)
    column = lambda s, c: (0, first + s)
    row = lambda s, c: (first + s, 0)
    block = lambda s, c: (lax.rem(s + count - c[1], count), 0)
    heads = count * STEP_HEADS
    parts_shape = jax.ShapeDtypeStruct((count * 2 * KVDIM, LATENT), BF16)
    parts_spec = pl.BlockSpec((2 * KVDIM, LATENT), block)
    dkeys_shape = keys.shape if is_last else (WIDE, n_keys)
    whole3 = lambda s, c: (0, 0, 0)
    held_specs = [
        pl.BlockSpec(memory_space=pltpu.VMEM),
        pl.BlockSpec(memory_space=pl.ANY),
        pl.BlockSpec(memory_space=pl.ANY),
    ]
    att, gq, keep, send, dkeys = pl.pallas_call(
        functools.partial(attend_kernel, scale=scale, is_first=is_first, is_last=is_last),
        grid_spec=pltpu.PrefetchScalarGridSpec(
            num_scalar_prefetch=1,
            grid=(count,),
            in_specs=[
                pl.BlockSpec(memory_space=pltpu.VMEM),
                pl.BlockSpec(memory_space=pltpu.VMEM),
                pl.BlockSpec((STEP_HEADS * tok, WIDE), row),
                pl.BlockSpec((STEP_HEADS * tok, LATENT), row),
                pl.BlockSpec((tok, STEP_HEADS * QDIM), column),
                pl.BlockSpec((tok, STEP_HEADS * VDIM), column),
                pl.BlockSpec((LATENT, STEP_HEADS * KVDIM), column),
            ] + held_specs[:len(held)],
            out_specs=[
                pl.BlockSpec((tok, STEP_HEADS * VDIM), column),
                pl.BlockSpec((tok, STEP_HEADS * QDIM), column),
                parts_spec,
                parts_spec,
                pl.BlockSpec(memory_space=pltpu.VMEM),
            ],
            scratch_shapes=[pltpu.VMEM((WIDE, n_keys), BF16)]
            + [pltpu.VMEM((WIDE, n_keys), F32)] * is_last,
        ),
        out_shape=[
            jax.ShapeDtypeStruct((tok, HEADS * VDIM), BF16),
            jax.ShapeDtypeStruct((tok, HEADS * QDIM), BF16),
            parts_shape,
            parts_shape,
            jax.ShapeDtypeStruct(dkeys_shape, BF16 if is_last else F32),
        ],
        input_output_aliases={9: 0, 10: 1} if held else {},
        compiler_params=pltpu.CompilerParams(vmem_limit_bytes=52 * 1024 * 1024),
        cost_estimate=pl.CostEstimate(
            flops=heads * 1_000_000_000, bytes_accessed=heads * 1_000_000, transcendentals=0
        ),
        name="attend",
    )(core, keys, bias, *absorbed, queries, grad_out, kv_weight, *held)
    return (dkeys, att, gq), keep, send


def table_lookup(lookup_table, positions):
    hits = positions[:, None] == jnp.arange(lookup_table.shape[0], dtype=jnp.int32)[None, :]
    return jnp.sum(jnp.where(hits, lookup_table[None, :], 0), axis=1)


def shifted(shard, axis, by):
    length = lax.axis_size(axis)
    pairs = [(i, i + by) for i in range(length) if 0 <= i + by < length]
    return lax.ppermute(shard, axis, pairs)


def body(queries, compressed, kv_weight, segments, grad_out):
    scale = QDIM ** (-0.5)
    tok = queries.shape[0]
    group = lax.axis_size("inner")
    n_outer = lax.axis_size("outer")
    inner = lax.axis_index("inner")
    outer = lax.axis_index("outer")
    own_block = outer * group + inner
    core = lax.rem(outer, 2)
    slots = jnp.arange(group, dtype=jnp.int32)
    own = compressed.T
    earlier = shifted(own, "outer", 1)
    outgoing = jnp.where((slots >= inner)[:, None, None], own[None], earlier[None])
    keys = lax.all_to_all(outgoing, "inner", split_axis=0, concat_axis=0, tiled=True)
    key_block = jnp.where(slots <= inner, outer * group + slots, (outer - 1) * group + slots)
    seg_keys = table_lookup(segments, key_block)
    seg_query = table_lookup(segments, own_block[None])
    slot_ok = (seg_keys == seg_query) & (key_block >= 0)
    at = jnp.arange(tok, dtype=jnp.int32)
    allowed = slot_ok[None, :, None] & (
        (slots != inner)[None, :, None] | (at[None, None, :] <= at[:, None, None])
    )
    bias = jnp.where(allowed, 0.0, -1e30).astype(F32).reshape(tok, group * tok)

    swap = [(o, o ^ 1) for o in range(n_outer)]
    row_y = lax.rem(lax.div(outer, 2), 4)

    def along_y(shard, by):
        return lax.ppermute(
            shard, "outer", [(o, o // 8 * 8 + (o % 8 + 2 * by) % 8) for o in range(n_outer)]
        )

    def summed(keep, send):
        other = lax.ppermute(send, "outer", swap)
        return (keep.astype(F32) + other.astype(F32)).astype(BF16)

    absorbed = absorb(queries, grad_out, kv_weight, scale)
    which = jnp.stack([core, jnp.zeros_like(core)])
    held, keep, send = attend_chunk(
        which, keys, bias, absorbed, queries, grad_out, kv_weight, (), 0, 4, scale
    )
    pair = summed(keep, send)
    which, pair = lax.optimization_barrier((jnp.stack([core, row_y]), pair))
    same_xc = [[x * 8 + y * 2 + c for y in range(4)] for x in range(2) for c in range(2)]
    first = lax.all_to_all(
        pair.reshape(4, 512, LATENT), "outer", split_axis=0, concat_axis=0,
        axis_index_groups=same_xc, tiled=True,
    )
    held, keep, send = attend_chunk(
        which, keys, bias, absorbed, queries, grad_out, kv_weight, held, 4, 4, scale
    )
    held, keep, send, first = lax.optimization_barrier((held, keep, send, first))
    dkeys, attended, grad_query = held
    other = lax.ppermute(send, "outer", swap)

    def piece(by):
        rows = slice(by * 512, (by + 1) * 512)
        return (keep[rows].astype(F32) + other[rows].astype(F32)).astype(BF16)

    moved = [along_y(piece(by), by) for by in (2, 1, 3)]
    arrived = lax.all_to_all(dkeys, "inner", split_axis=0, concat_axis=0, tiled=True)
    own_piece, first, arrived = lax.optimization_barrier((piece(0), first, arrived))
    second = sum(m.astype(F32) for m in moved) + own_piece.astype(F32)

    def along_inner(part):
        part = part.astype(BF16).reshape(group, 64, LATENT)
        part = lax.all_to_all(part, "inner", split_axis=0, concat_axis=0, tiled=True)
        return jnp.sum(part.astype(F32), axis=0)

    arrived = arrived.astype(F32)
    from_group = (slots >= inner)[:, None, None]
    own_term = jnp.sum(jnp.where(from_group, arrived, 0.0), axis=0)
    later_term = jnp.sum(jnp.where(from_group, 0.0, arrived), axis=0)
    next_term = shifted(later_term.astype(BF16), "outer", -1).astype(F32)
    grad_compressed = (own_term + next_term).astype(BF16).T

    first = along_inner(jnp.sum(first.astype(F32), axis=0))
    second = along_inner(second)
    low = outer < 8
    crossing = jnp.where(low, second, first).astype(BF16)
    crossing = lax.ppermute(crossing, "outer", [(o, o ^ 8) for o in range(n_outer)])
    grad_weight_t = jnp.where(low, first, second) + crossing.astype(F32)
    return attended, grad_query, grad_compressed, grad_weight_t


def solution(mesh):
    return jax.shard_map(
        body,
        mesh=mesh,
        in_specs=(
            P(("outer", "inner"), None),
            P(("outer", "inner"), None),
            P(),
            P(),
            P(("outer", "inner"), None),
        ),
        out_specs=(
            P(("outer", "inner"), None),
            P(("outer", "inner"), None),
            P(("outer", "inner"), None),
            P(("outer", "inner"), None),
        ),
        check_vma=False,
    )
```

```python
import functools

import jax
import jax.numpy as jnp
from jax import lax
from jax.experimental import pallas as pl
from jax.experimental.pallas import tpu as pltpu
from jax.sharding import PartitionSpec as P

LATENT = 512
NOPE = 128
ROPE = 64
VDIM = 128
HEADS = 32
TILE = 128
QDIM = NOPE + ROPE
KVDIM = NOPE + VDIM
WIDE = LATENT + ROPE
STEP_HEADS = 4
CHUNKS = ((0, 4), (4, 4))
BF16 = jnp.bfloat16
F32 = jnp.float32

ROWS_ROWS = (((1,), (1,)), ((), ()))
COLS_COLS = (((0,), (0,)), ((), ()))


def dot(a, b):
    return jnp.dot(a, b, preferred_element_type=F32)


def dot_general(a, b, dims):
    return lax.dot_general(a, b, dims, preferred_element_type=F32)


def absorb_kernel(q_ref, g_ref, w_ref, qc_ref, ga_ref, *, scale):
    tok = q_ref.shape[0]
    for h in range(STEP_HEADS):
        rows = slice(h * tok, (h + 1) * tok)
        q_nope = q_ref[:, h * QDIM:h * QDIM + NOPE]
        q_rope = q_ref[:, h * QDIM + NOPE:(h + 1) * QDIM]
        key_weight = w_ref[:, h * KVDIM:h * KVDIM + NOPE]
        value_weight = w_ref[:, h * KVDIM + NOPE:(h + 1) * KVDIM]
        qc_ref[rows, :LATENT] = (dot_general(q_nope, key_weight, ROWS_ROWS) * scale).astype(BF16)
        qc_ref[rows, LATENT:] = (q_rope.astype(F32) * scale).astype(BF16)
        grad_head = g_ref[:, h * VDIM:(h + 1) * VDIM]
        ga_ref[rows] = dot_general(grad_head, value_weight, ROWS_ROWS).astype(BF16)


def absorb(queries, grad_out, kv_weight, scale):
    tok = queries.shape[0]
    rows = STEP_HEADS * tok
    column = lambda s: (0, s)
    row = lambda s: (s, 0)
    return pl.pallas_call(
        functools.partial(absorb_kernel, scale=scale),
        grid=(HEADS // STEP_HEADS,),
        in_specs=[
            pl.BlockSpec((tok, STEP_HEADS * QDIM), column),
            pl.BlockSpec((tok, STEP_HEADS * VDIM), column),
            pl.BlockSpec((LATENT, STEP_HEADS * KVDIM), column),
        ],
        out_specs=[pl.BlockSpec((rows, WIDE), row), pl.BlockSpec((rows, LATENT), row)],
        out_shape=[
            jax.ShapeDtypeStruct((HEADS * tok, WIDE), BF16),
            jax.ShapeDtypeStruct((HEADS * tok, LATENT), BF16),
        ],
        compiler_params=pltpu.CompilerParams(vmem_limit_bytes=24 * 1024 * 1024),
        cost_estimate=pl.CostEstimate(
            flops=6_000_000_000, bytes_accessed=20_000_000, transcendentals=0
        ),
        name="absorb",
    )(queries, grad_out, kv_weight)


def attend_kernel(core_ref, keys_ref, bias_ref, qc_ref, ga_ref, q_ref, g_ref, w_ref, *rest, scale, is_first, is_last):
    att_ref, gq_ref, keep_ref, send_ref, dkeys_ref, keys_t_ref, *acc = rest if is_first else rest[3:]
    acc_ref = acc[0] if is_last else dkeys_ref
    tok = q_ref.shape[0]
    slots = keys_ref.shape[0]

    @pl.when(pl.program_id(0) == 0)
    def _():
        acc_ref[...] = jnp.zeros_like(acc_ref) if is_first else rest[0][...]
        for s in range(slots):
            keys_t_ref[:, s * tok:(s + 1) * tok] = keys_ref[s]

    def q_nope(h):
        return q_ref[:, h * QDIM:h * QDIM + NOPE]

    def grad_head(h):
        return g_ref[:, h * VDIM:(h + 1) * VDIM]

    def key_weight(h):
        return w_ref[:, h * KVDIM:h * KVDIM + NOPE]

    def value_weight(h):
        return w_ref[:, h * KVDIM + NOPE:(h + 1) * KVDIM]

    keys_t = keys_t_ref[...]
    latent_t = keys_t_ref[:LATENT]
    q_cat = qc_ref[...]
    g_abs = ga_ref[...]
    scores = dot(q_cat, keys_t)
    grad_probs = dot(g_abs, latent_t)
    bias = bias_ref[...]
    probs_half, grad_scores = [], []
    for h in range(STEP_HEADS):
        s = scores[h * tok:(h + 1) * tok] + bias
        s = jnp.exp(s - jnp.max(s, axis=1, keepdims=True))
        p = s * (1.0 / jnp.sum(s, axis=1, keepdims=True))
        gp = grad_probs[h * tok:(h + 1) * tok]
        row_dot = jnp.sum(p * gp, axis=1, keepdims=True)
        probs_half.append(p.astype(BF16))
        grad_scores.append((p * (gp - row_dot)).astype(BF16))
    probs_half = jnp.concatenate(probs_half, axis=0)
    grad_scores = jnp.concatenate(grad_scores, axis=0)
    acc_ref[:LATENT] += dot_general(q_cat[:, :LATENT], grad_scores, COLS_COLS) + dot_general(
        g_abs, probs_half, COLS_COLS
    )
    acc_ref[LATENT:] += dot_general(q_cat[:, LATENT:], grad_scores, COLS_COLS)
    mixed = dot_general(probs_half, latent_t, ROWS_ROWS).astype(BF16)
    grad_mixed = dot_general(grad_scores, keys_t, ROWS_ROWS) * scale
    grad_mixed_lat = grad_mixed[:, :LATENT].astype(BF16)
    grad_rope = grad_mixed[:, LATENT:].astype(BF16)
    terms = []
    for h in range(STEP_HEADS):
        rows = slice(h * tok, (h + 1) * tok)
        att_ref[:, h * VDIM:(h + 1) * VDIM] = dot(mixed[rows], value_weight(h)).astype(BF16)
        gq_ref[:, h * QDIM:h * QDIM + NOPE] = dot(grad_mixed_lat[rows], key_weight(h)).astype(BF16)
        gq_ref[:, h * QDIM + NOPE:(h + 1) * QDIM] = grad_rope[rows]
        key_term = dot_general(q_nope(h), grad_mixed_lat[rows], COLS_COLS).astype(BF16)
        value_term = dot_general(grad_head(h), mixed[rows], COLS_COLS).astype(BF16)
        terms.append((key_term, value_term))

    def put(ref, heads):
        for n, head in enumerate(heads):
            ref[n * KVDIM:n * KVDIM + NOPE] = terms[head][0]
            ref[n * KVDIM + NOPE:(n + 1) * KVDIM] = terms[head][1]

    @pl.when(core_ref[0] == 0)
    def _():
        put(keep_ref, (0, 1))
        put(send_ref, (2, 3))

    @pl.when(core_ref[0] != 0)
    def _():
        put(keep_ref, (2, 3))
        put(send_ref, (0, 1))

    if is_last:
        @pl.when(pl.program_id(0) == pl.num_programs(0) - 1)
        def _():
            for s in range(slots):
                dkeys_ref[s] = acc_ref[:, s * tok:(s + 1) * tok].astype(BF16)


def attend_chunk(core, keys, bias, absorbed, queries, grad_out, kv_weight, held, first, count, scale):
    tok = queries.shape[0]
    slots = keys.shape[0]
    n_keys = slots * tok
    is_first, is_last = first == 0, (first + count) * STEP_HEADS == HEADS
    whole = lambda s, c: (0, 0)
    column = lambda s, c: (0, first + s)
    row = lambda s, c: (first + s, 0)
    block = lambda s, c: (lax.rem(s + count - c[1], count), 0)
    heads = count * STEP_HEADS
    parts_shape = jax.ShapeDtypeStruct((count * 2 * KVDIM, LATENT), BF16)
    parts_spec = pl.BlockSpec((2 * KVDIM, LATENT), block)
    dkeys_shape = keys.shape if is_last else (WIDE, n_keys)
    whole3 = lambda s, c: (0, 0, 0)
    held_specs = [
        pl.BlockSpec(memory_space=pltpu.VMEM),
        pl.BlockSpec(memory_space=pl.ANY),
        pl.BlockSpec(memory_space=pl.ANY),
    ]
    att, gq, keep, send, dkeys = pl.pallas_call(
        functools.partial(attend_kernel, scale=scale, is_first=is_first, is_last=is_last),
        grid_spec=pltpu.PrefetchScalarGridSpec(
            num_scalar_prefetch=1,
            grid=(count,),
            in_specs=[
                pl.BlockSpec(memory_space=pltpu.VMEM),
                pl.BlockSpec(memory_space=pltpu.VMEM),
                pl.BlockSpec((STEP_HEADS * tok, WIDE), row),
                pl.BlockSpec((STEP_HEADS * tok, LATENT), row),
                pl.BlockSpec((tok, STEP_HEADS * QDIM), column),
                pl.BlockSpec((tok, STEP_HEADS * VDIM), column),
                pl.BlockSpec((LATENT, STEP_HEADS * KVDIM), column),
            ] + held_specs[:len(held)],
            out_specs=[
                pl.BlockSpec((tok, STEP_HEADS * VDIM), column),
                pl.BlockSpec((tok, STEP_HEADS * QDIM), column),
                parts_spec,
                parts_spec,
                pl.BlockSpec(memory_space=pltpu.VMEM),
            ],
            scratch_shapes=[pltpu.VMEM((WIDE, n_keys), BF16)]
            + [pltpu.VMEM((WIDE, n_keys), F32)] * is_last,
        ),
        out_shape=[
            jax.ShapeDtypeStruct((tok, HEADS * VDIM), BF16),
            jax.ShapeDtypeStruct((tok, HEADS * QDIM), BF16),
            parts_shape,
            parts_shape,
            jax.ShapeDtypeStruct(dkeys_shape, BF16 if is_last else F32),
        ],
        input_output_aliases={9: 0, 10: 1} if held else {},
        compiler_params=pltpu.CompilerParams(vmem_limit_bytes=52 * 1024 * 1024),
        cost_estimate=pl.CostEstimate(
            flops=heads * 1_000_000_000, bytes_accessed=heads * 1_000_000, transcendentals=0
        ),
        name="attend",
    )(core, keys, bias, *absorbed, queries, grad_out, kv_weight, *held)
    return (dkeys, att, gq), keep, send


def table_lookup(lookup_table, positions):
    hits = positions[:, None] == jnp.arange(lookup_table.shape[0], dtype=jnp.int32)[None, :]
    return jnp.sum(jnp.where(hits, lookup_table[None, :], 0), axis=1)


def shifted(shard, axis, by):
    length = lax.axis_size(axis)
    pairs = [(i, i + by) for i in range(length) if 0 <= i + by < length]
    return lax.ppermute(shard, axis, pairs)


def body(queries, compressed, kv_weight, segments, grad_out):
    scale = QDIM ** (-0.5)
    tok = queries.shape[0]
    group = lax.axis_size("inner")
    n_outer = lax.axis_size("outer")
    inner = lax.axis_index("inner")
    outer = lax.axis_index("outer")
    own_block = outer * group + inner
    core = lax.rem(outer, 2)
    slots = jnp.arange(group, dtype=jnp.int32)
    own = compressed.T
    earlier = shifted(own, "outer", 1)
    outgoing = jnp.where((slots >= inner)[:, None, None], own[None], earlier[None])
    keys = lax.all_to_all(outgoing, "inner", split_axis=0, concat_axis=0, tiled=True)
    key_block = jnp.where(slots <= inner, outer * group + slots, (outer - 1) * group + slots)
    seg_keys = table_lookup(segments, key_block)
    seg_query = table_lookup(segments, own_block[None])
    slot_ok = (seg_keys == seg_query) & (key_block >= 0)
    at = jnp.arange(tok, dtype=jnp.int32)
    allowed = slot_ok[None, :, None] & (
        (slots != inner)[None, :, None] | (at[None, None, :] <= at[:, None, None])
    )
    bias = jnp.where(allowed, 0.0, -1e30).astype(F32).reshape(tok, group * tok)

    swap = [(o, o ^ 1) for o in range(n_outer)]
    row_y = lax.rem(lax.div(outer, 2), 4)

    def along_y(shard, by):
        return lax.ppermute(
            shard, "outer", [(o, o // 8 * 8 + (o % 8 + 2 * by) % 8) for o in range(n_outer)]
        )

    def summed(keep, send):
        other = lax.ppermute(send, "outer", swap)
        return (keep.astype(F32) + other.astype(F32)).astype(BF16)

    absorbed = absorb(queries, grad_out, kv_weight, scale)
    which = jnp.stack([core, jnp.zeros_like(core)])
    held, keep, send = attend_chunk(
        which, keys, bias, absorbed, queries, grad_out, kv_weight, (), 0, 4, scale
    )
    pair = summed(keep, send)
    which, pair = lax.optimization_barrier((jnp.stack([core, row_y]), pair))
    same_xc = [[x * 8 + y * 2 + c for y in range(4)] for x in range(2) for c in range(2)]
    first = lax.all_to_all(
        pair.reshape(4, 512, LATENT), "outer", split_axis=0, concat_axis=0,
        axis_index_groups=same_xc, tiled=True,
    )
    held, keep, send = attend_chunk(
        which, keys, bias, absorbed, queries, grad_out, kv_weight, held, 4, 4, scale
    )
    held, keep, send, first = lax.optimization_barrier((held, keep, send, first))
    dkeys, attended, grad_query = held
    other = lax.ppermute(send, "outer", swap)

    def piece(by):
        rows = slice(by * 512, (by + 1) * 512)
        return (keep[rows].astype(F32) + other[rows].astype(F32)).astype(BF16)

    moved = [along_y(piece(by), by) for by in (2, 1, 3)]
    arrived = lax.all_to_all(dkeys, "inner", split_axis=0, concat_axis=0, tiled=True)
    own_piece, first = lax.optimization_barrier((piece(0), first))
    first = jnp.sum(first.astype(F32), axis=0).astype(BF16)
    own_piece, first, arrived = lax.optimization_barrier((own_piece, first, arrived))
    second = sum(m.astype(F32) for m in moved) + own_piece.astype(F32)

    def along_inner(part):
        part = part.astype(BF16).reshape(group, 64, LATENT)
        part = lax.all_to_all(part, "inner", split_axis=0, concat_axis=0, tiled=True)
        return jnp.sum(part.astype(F32), axis=0)

    arrived = arrived.astype(F32)
    from_group = (slots >= inner)[:, None, None]
    own_term = jnp.sum(jnp.where(from_group, arrived, 0.0), axis=0)
    later_term = jnp.sum(jnp.where(from_group, 0.0, arrived), axis=0)
    next_term = shifted(later_term.astype(BF16), "outer", -1).astype(F32)
    grad_compressed = (own_term + next_term).astype(BF16).T

    first = along_inner(first)
    second = along_inner(second)
    low = outer < 8
    crossing = jnp.where(low, second, first).astype(BF16)
    crossing = lax.ppermute(crossing, "outer", [(o, o ^ 8) for o in range(n_outer)])
    grad_weight_t = jnp.where(low, first, second) + crossing.astype(F32)
    return attended, grad_query, grad_compressed, grad_weight_t


def solution(mesh):
    return jax.shard_map(
        body,
        mesh=mesh,
        in_specs=(
            P(("outer", "inner"), None),
            P(("outer", "inner"), None),
            P(),
            P(),
            P(("outer", "inner"), None),
        ),
        out_specs=(
            P(("outer", "inner"), None),
            P(("outer", "inner"), None),
            P(("outer", "inner"), None),
            P(("outer", "inner"), None),
        ),
        check_vma=False,
    )
```
